128 devices in a mesh: dp: 32 (over y, z, core), cent: 4 (over x).
Axes of the slice: x: 4, y: 4, z: 4, core: 2. Of those that a mesh axis runs over, the one named last changes fastest.
Arguments:
- embeddings: bfloat16 [32768, 1024], P('dp'), may hold values from -8 to 8, as said below
- centroids: bfloat16 [16384, 1024], P('cent'), may hold values from -0.125 to 0.125, as said below
Outputs:
- log_norm: float32 [32768], P('dp')
- new_centroids: bfloat16 [16384, 1024], P('cent', 'dp')
The draws below stay inside these ranges and needn't reach their ends.
Inputs may be any that keep to these rules, and one draw needn't show every extreme that they name: Real-valued embeddings. Real-valued centroids.
All inputs are finite; a program needn't handle non-finite values.
Results may differ from the reference program's by a relative error of at most 0.006.
Values may be sent and summed in bfloat16 or wider, within the bound.
A program may use at most 128 MiB of HBM per device.

```python
import math
import jax
import jax.numpy as jnp
from jax import lax

D = 1024
K = 16384
ROWS_DEV = 1024
ROWS = 32768
N_DP = 32


def shared_centres(key):
    own_key = jax.random.fold_in(key, 11)
    drawn = jax.random.normal(own_key, (K, D), dtype=jnp.float32)
    return jnp.clip(drawn, -4.0, 4.0) / math.sqrt(D)


def draw_centroids(key, part):
    centres = shared_centres(key)
    return centres.astype(jnp.bfloat16)


def draw_embeddings(key, part):
    centres = shared_centres(key)
    key = jax.random.fold_in(key, 5)
    subkeys = jax.random.split(key, 8)
    limit = 8.0 if D >= 1024 else 32.0
    picked = jax.random.randint(subkeys[2], (ROWS,), 0, 16) == 0
    forced = jnp.arange(ROWS) == jax.random.randint(subkeys[7], (), 0, ROWS)
    chosen = jnp.logical_or(picked, forced)
    leader = jax.random.randint(subkeys[3], (ROWS,), 0, K)
    runner = (leader + jax.random.randint(subkeys[4], (ROWS,), 1, K)) % K
    strength = 60.0 + 30.0 * jax.random.randint(subkeys[5], (ROWS,), 0, 3).astype(jnp.float32)
    gap_size = jax.random.uniform(subkeys[6], (ROWS,), jnp.float32, 0.5, 1.5)
    aligned = strength[:, None] * centres[leader] + (strength - gap_size)[:, None] * centres[runner]
    aligned = jnp.clip(aligned, -limit, limit)
    drawn_rows = jnp.clip(jax.random.normal(subkeys[0], (ROWS, D), dtype=jnp.float32), -6.0, 6.0)
    rows_out = jnp.where(chosen[:, None], aligned, drawn_rows)
    return rows_out.astype(jnp.bfloat16)


def setup_inputs(seed: int = 0) -> dict:
    arg_keys = jax.random.split(jax.random.key(seed), 3)
    return {
        "embeddings": draw_embeddings(jax.random.fold_in(arg_keys[2], 71), 0),
        "centroids": draw_centroids(jax.random.fold_in(arg_keys[2], 71), 0),
    }


sharpness = 2.0
pseudo_count = 1.0


def reference(embeddings, centroids):
    blocks = embeddings.reshape(N_DP, ROWS_DEV, D)

    def step(carry, block_rows):
        weighted, mass = carry
        scores = sharpness * jnp.dot(block_rows, centroids.T, preferred_element_type=jnp.float32)
        row_max = jnp.max(scores, axis=1)
        row_total = jnp.sum(jnp.exp(scores - row_max[:, None]), axis=1)
        norm_rows = row_max + jnp.log(row_total)
        resp = jnp.exp(scores - norm_rows[:, None]).astype(jnp.bfloat16)
        weighted = weighted + jnp.dot(resp.T, block_rows, preferred_element_type=jnp.float32)
        mass = mass + jnp.sum(resp.astype(jnp.float32), axis=0)
        return (weighted, mass), norm_rows

    start = (jnp.zeros((K, D), jnp.float32), jnp.zeros((K,), jnp.float32))
    (weighted, mass), norms = lax.scan(step, start, blocks)
    updated = (weighted + pseudo_count * centroids.astype(jnp.float32)) / (mass + pseudo_count)[:, None]
    return norms.reshape(ROWS), updated.astype(jnp.bfloat16)
```

```python
import jax
import jax.numpy as jnp
from jax import lax
from jax.experimental import pallas as pl
from jax.experimental.pallas import tpu as pltpu
from jax.sharding import PartitionSpec as P

MESH = pl.DeviceIdType.MESH
F32, BF16 = jnp.float32, jnp.bfloat16

SIDE = 4
D = 1024
ROWS = 1024
CENT = 4096
HALF = CENT // 2
BLOCK = 256
CHUNK = 256
N_BLOCKS = 2 * ROWS // BLOCK
N_CHUNKS = HALF // CHUNK
CHIP_COLS = D // (SIDE * SIDE)
DEV_COLS = CHIP_COLS // 2

OTHERS = [(d, c) for c in range(2) for d in range(SIDE) if (d, c) != (0, 0)]


def kernel(
    e_hbm, c_hbm, norm_ref, out_ref,
    emb, emb2, emb_t, cent, scores, resp, weighted, relay, gather_a, gather_b, second, gather_c, previous,
    lse, lse_in, norm_row, mass, mass_in, mass_y, mass_in2, den,
    load_sem, emb_send, emb_recv, lse_send, lse_recv, a_send, a_recv, b_send, b_recv, c_send, c_recv,
    mass_send, mass_recv,
):
    dp = lax.axis_index("dp")
    x = lax.axis_index("cent")
    y, z, core = dp // 8, lax.rem(dp // 2, SIDE), lax.rem(dp, 2)

    def device(dx, dy, dz, dc):
        return {
            "dp": (lax.rem(y + dy, SIDE) * SIDE + lax.rem(z + dz, SIDE)) * 2 + lax.rem(core + dc, 2),
            "cent": lax.rem(x + dx, SIDE),
        }

    def along(axis, d, dc):
        return device(*[d if a == axis else 0 for a in range(3)], dc)

    def send(src, dst, send_sem, recv_sem, target):
        pltpu.make_async_remote_copy(
            src_ref=src, dst_ref=dst, send_sem=send_sem, recv_sem=recv_sem, device_id=target, device_id_type=MESH
        ).start()

    def wait(ref, sem):
        pltpu.make_async_copy(ref, ref, sem).wait()

    e_loads = [
        pltpu.make_async_copy(e_hbm.at[pl.ds(b * BLOCK, BLOCK)], emb.at[0, pl.ds(b * BLOCK, BLOCK)], load_sem.at[b])
        for b in range(4)
    ]
    c_loads = [
        pltpu.make_async_copy(
            c_hbm.at[pl.ds(core * HALF + m * 512, 512)], cent.at[0, pl.ds(m * 512, 512)], load_sem.at[4 + m]
        )
        for m in range(4)
    ]
    c_other = pltpu.make_async_copy(c_hbm.at[pl.ds((1 - core) * HALF, HALF)], cent.at[1], load_sem.at[8])
    for copy in [e_loads[0], *c_loads, *e_loads[1:], c_other]:
        copy.start()

    barrier = pltpu.get_barrier_semaphore()
    for d, dc in OTHERS:
        for axis in range(3):
            if d or axis == 0:
                pl.semaphore_signal(barrier, inc=1, device_id=along(axis, d, dc), device_id_type=MESH)

    def statistics(b):
        ref = scores.at[b]
        top = ref[0:64].reshape(8, 8, BLOCK).max(0)
        for j in range(64, HALF, 64):
            top = jnp.maximum(top, ref[j : j + 64].reshape(8, 8, BLOCK).max(0))
        top = jnp.max(top, axis=0, keepdims=True)
        total = jnp.zeros((8, BLOCK), F32)
        for j in range(0, HALF, 64):
            total = total + jnp.exp(ref[j : j + 64] - top).reshape(8, 8, BLOCK).sum(0)
        value = top + jnp.log(jnp.sum(total, axis=0, keepdims=True))
        group, row = b // 4, 2 * (b % 4)
        lse[group, row : row + 1] = value[:, 0:128]
        lse[group, row + 1 : row + 2] = value[:, 128:256]

    def send_lse(group):
        for j, (d, dc) in enumerate(OTHERS):
            send(lse.at[group], lse_in.at[group ^ dc, j], lse_send, lse_recv.at[group ^ dc], along(0, d, dc))

    emb_t[D : D + 16, :] = jnp.ones((16, 2 * ROWS), BF16)
    for b in range(N_BLOCKS):
        slot, first = b // 4, (b % 4) * BLOCK
        if b < 3:
            e_loads[b].wait()
        elif b >= 4 and b % 2 == 0:
            wait(emb.at[1, pl.ds(first, 512)], emb_recv.at[b // 2 - 2])
        rows = emb[slot, first : first + BLOCK]
        emb2[...] = rows * BF16(2)
        for m in range(HALF // 512):
            if b == 0:
                c_loads[m].wait()
            scores[b, m * 512 : m * 512 + 512] = lax.dot_general(
                cent[0, m * 512 : m * 512 + 512], emb2[...], (((1,), (1,)), ((), ())), preferred_element_type=F32
            )
        emb_t[0:D, b * BLOCK : (b + 1) * BLOCK] = rows.T
        if b:
            statistics(b - 1)
        if b == 2:
            e_loads[3].wait()
            pl.semaphore_wait(barrier, 19)
            for h in range(2):
                part = pl.ds(h * 512, 512)
                send(emb.at[0, part], emb.at[1, part], emb_send, emb_recv.at[h], device(0, 0, 0, 1))
        if b == 4:
            send_lse(0)
    statistics(N_BLOCKS - 1)
    send_lse(1)

    for group in range(2):
        wait(lse_in.at[group], lse_recv.at[group])
        parts = [lse[group]] + [lse_in[group, j] for j in range(7)]
        top = parts[0]
        for part in parts[1:]:
            top = jnp.maximum(top, part)
        total = jnp.zeros_like(top)
        for part in parts:
            total = total + jnp.exp(part - top)
        norm = top + jnp.log(total)
        if group == 0:
            norm_ref[...] = norm
        for j in range(8):
            at = group * ROWS + j * 128
            norm_row[0:1, at : at + 128] = norm[j : j + 1]

    def exponentials(i):
        for b in range(N_BLOCKS):
            norm = norm_row[0:1, b * BLOCK : (b + 1) * BLOCK]
            for j in range(0, CHUNK, 32):
                at = i * CHUNK + j
                resp[i % 2, j : j + 32, b * BLOCK : (b + 1) * BLOCK] = jnp.exp(
                    scores[b, at : at + 32] - norm
                ).astype(BF16)

    def product(i):
        sums = lax.dot_general(
            emb_t[...], resp[i % 2], (((1,), (1,)), ((), ())), preferred_element_type=F32
        )
        for yy in range(SIDE):
            for zz in range(SIDE):
                at = (yy * SIDE + zz) * CHIP_COLS
                value = sums[at : at + CHIP_COLS].astype(BF16)
                if i % 2 == 0:
                    weighted[i, yy, zz] = value
                else:
                    weighted[i, zz, yy] = value
        mass[2 * i : 2 * i + 1] = sums[D : D + 1, 0:128]
        mass[2 * i + 1 : 2 * i + 2] = sums[D : D + 1, 128:256]

    def places(i):
        return (1, y, 2, z) if i % 2 == 0 else (2, z, 1, y)

    def send_a(i):
        axis, p, _, _ = places(i)
        up, down, far = lax.rem(p + 1, SIDE), lax.rem(p + 3, SIDE), lax.rem(p + 2, SIDE)
        to_up, to_down = along(axis, 1, 0), along(axis, 3, 0)
        lo, hi = pl.ds(0, 2), pl.ds(2, 2)
        send(weighted.at[i, far, lo], gather_a.at[i, 0, 0], a_send, a_recv.at[i, 0], to_up)
        send(weighted.at[i, far, hi], gather_a.at[i, 0, 1], a_send, a_recv.at[i, 0], to_down)
        send(weighted.at[i, up, hi], gather_a.at[i, 1, 0], a_send, a_recv.at[i, 1], to_up)
        send(weighted.at[i, down, lo], gather_a.at[i, 1, 1], a_send, a_recv.at[i, 1], to_down)

    def send_b(i):
        axis, p, _, _ = places(i)
        up, down = lax.rem(p + 1, SIDE), lax.rem(p + 3, SIDE)
        wait(gather_a.at[i, 0], a_recv.at[i, 0])
        relay[i, 0] = (weighted[i, up, 0:2].astype(F32) + gather_a[i, 0, 0].astype(F32)).astype(BF16)
        relay[i, 1] = (weighted[i, down, 2:4].astype(F32) + gather_a[i, 0, 1].astype(F32)).astype(BF16)
        send(relay.at[i, 0], gather_b.at[i, 0], b_send, b_recv.at[i], along(axis, 1, 0))
        send(relay.at[i, 1], gather_b.at[i, 1], b_send, b_recv.at[i], along(axis, 3, 0))

    def send_c(i):
        _, p, axis, q = places(i)
        wait(gather_a.at[i, 1], a_recv.at[i, 1])
        wait(gather_b.at[i], b_recv.at[i])
        low = weighted[i, p, 0:2].astype(F32) + gather_b[i, 0].astype(F32) + gather_a[i, 1, 1].astype(F32)
        high = weighted[i, p, 2:4].astype(F32) + gather_b[i, 1].astype(F32) + gather_a[i, 1, 0].astype(F32)
        second[i, 0:2] = low.astype(BF16).reshape(2, 2, DEV_COLS, CHUNK)
        second[i, 2:4] = high.astype(BF16).reshape(2, 2, DEV_COLS, CHUNK)
        for j, (d, dc) in enumerate(OTHERS):
            send(
                second.at[i, lax.rem(q + d, SIDE), lax.rem(core + dc, 2)], gather_c.at[i, j],
                c_send, c_recv.at[i], along(axis, d, dc),
            )

    def finish(i):
        _, _, _, q = places(i)
        wait(gather_c.at[i], c_recv.at[i])
        at = slice(i * CHUNK, (i + 1) * CHUNK)
        for h in range(2):
            if h == 0:
                total = second[i, q, core].astype(F32)
                for j in range(3):
                    total = total + gather_c[i, j].astype(F32)
            else:
                total = gather_c[i, 3].astype(F32)
                for j in range(4, 7):
                    total = total + gather_c[i, j].astype(F32)
            total = total + previous[h, :, at]
            for k in range(2):
                part = slice(k * 128, (k + 1) * 128)
                out_ref[lax.rem(core + h, 2), :, i * CHUNK + k * 128 : i * CHUNK + (k + 1) * 128] = (
                    total[:, part] / den[h, 2 * i + k : 2 * i + k + 1]
                ).astype(BF16)

    exponentials(0)
    for i in range(N_CHUNKS):
        product(i)
        if i + 1 < N_CHUNKS:
            exponentials(i + 1)
        send_a(i)

    for d in range(1, SIDE):
        send(mass, mass_in.at[d - 1], mass_send, mass_recv.at[0], along(1, d, 0))

    c_other.wait()
    row = lax.broadcasted_iota(jnp.int32, (DEV_COLS, D), 0)
    col = lax.broadcasted_iota(jnp.int32, (DEV_COLS, D), 1)
    pick = jnp.where(col == row + dp * DEV_COLS, 1.0, 0.0).astype(BF16)
    for h in range(2):
        for m in range(0, HALF, 512):
            previous[h, :, m : m + 512] = lax.dot_general(
                pick, cent[h, m : m + 512], (((1,), (1,)), ((), ())), preferred_element_type=F32
            )

    for i in range(4):
        send_b(i)
    wait(mass_in, mass_recv.at[0])
    mass_y[...] = mass[...] + mass_in[0] + mass_in[1] + mass_in[2]
    for j, (d, dc) in enumerate(OTHERS):
        send(mass_y, mass_in2.at[j], mass_send, mass_recv.at[1], along(2, d, dc))
    for i in range(4):
        send_b(i + 4)
        send_c(i)
    wait(mass_in2, mass_recv.at[1])
    den[0] = mass_y[...] + mass_in2[0] + mass_in2[1] + mass_in2[2] + 1.0
    den[1] = mass_in2[3] + mass_in2[4] + mass_in2[5] + mass_in2[6] + 1.0
    for i in range(4):
        send_c(i + 4)
        finish(i)
    wait(emb.at[1], emb_send)
    wait(lse_in, lse_send)
    wait(gather_a, a_send)
    wait(gather_b, b_send)
    wait(mass_in, mass_send)
    wait(mass_in2, mass_send)
    wait(gather_c, c_send)
    for i in range(4, N_CHUNKS):
        finish(i)


def per_device(embeddings, centroids):
    dma = pltpu.SemaphoreType.DMA
    norm, out = pl.pallas_call(
        kernel,
        out_shape=(
            jax.ShapeDtypeStruct((8, 128), F32),
            jax.ShapeDtypeStruct((2, DEV_COLS, HALF), BF16),
        ),
        in_specs=[pl.BlockSpec(memory_space=pl.ANY)] * 2,
        out_specs=(pl.BlockSpec(memory_space=pltpu.VMEM),) * 2,
        scratch_shapes=[
            pltpu.VMEM((2, ROWS, D), BF16),
            pltpu.VMEM((BLOCK, D), BF16),
            pltpu.VMEM((D + 16, 2 * ROWS), BF16),
            pltpu.VMEM((2, HALF, D), BF16),
            pltpu.VMEM((N_BLOCKS, HALF, BLOCK), F32),
            pltpu.VMEM((2, CHUNK, 2 * ROWS), BF16),
            pltpu.VMEM((N_CHUNKS, SIDE, SIDE, CHIP_COLS, CHUNK), BF16),
            pltpu.VMEM((N_CHUNKS, 2, 2, CHIP_COLS, CHUNK), BF16),
            pltpu.VMEM((N_CHUNKS, 2, 2, 2, CHIP_COLS, CHUNK), BF16),
            pltpu.VMEM((N_CHUNKS, 2, 2, CHIP_COLS, CHUNK), BF16),
            pltpu.VMEM((N_CHUNKS, SIDE, 2, DEV_COLS, CHUNK), BF16),
            pltpu.VMEM((N_CHUNKS, 7, DEV_COLS, CHUNK), BF16),
            pltpu.VMEM((2, DEV_COLS, HALF), F32),
            pltpu.VMEM((2, 8, 128), F32),
            pltpu.VMEM((2, 7, 8, 128), F32),
            pltpu.VMEM((1, 2 * ROWS), F32),
            pltpu.VMEM((16, 128), F32),
            pltpu.VMEM((3, 16, 128), F32),
            pltpu.VMEM((16, 128), F32),
            pltpu.VMEM((7, 16, 128), F32),
            pltpu.VMEM((2, 16, 128), F32),
            dma((9,)),
            dma, dma((2,)),
            dma, dma((2,)),
            dma, dma((N_CHUNKS, 2)),
            dma, dma((N_CHUNKS,)),
            dma, dma((N_CHUNKS,)),
            dma, dma((2,)),
        ],
        compiler_params=pltpu.CompilerParams(
            collective_id=0, has_side_effects=True, vmem_limit_bytes=60 * 2**20
        ),
    )(embeddings, centroids)
    return norm.reshape(ROWS), out.transpose(0, 2, 1).reshape(CENT, DEV_COLS)


def solution(mesh):
    return jax.shard_map(
        per_device,
        mesh=mesh,
        in_specs=(P("dp", None), P("cent", None)),
        out_specs=(P("dp"), P("cent", "dp")),
        check_vma=False,
    )
```

```python
import jax
import jax.numpy as jnp
from jax import lax
from jax.experimental import pallas as pl
from jax.experimental.pallas import tpu as pltpu
from jax.sharding import PartitionSpec as P

MESH = pl.DeviceIdType.MESH
F32, BF16 = jnp.float32, jnp.bfloat16

SIDE = 4
D = 1024
ROWS = 1024
CENT = 4096
HALF = CENT // 2
BLOCK = 256
TILE = 256
CHUNK = 256
N_BLOCKS = 2 * ROWS // BLOCK
N_CHUNKS = HALF // CHUNK
CHIP_COLS = D // (SIDE * SIDE)
DEV_COLS = CHIP_COLS // 2

OTHERS = [(d, c) for c in range(2) for d in range(SIDE) if (d, c) != (0, 0)]


def kernel(
    e_hbm, c_hbm, norm_ref, out_ref,
    emb, emb2, emb_t, cent, scores, resp, weighted, relay, gather_a, gather_b, second, gather_c, previous,
    lse, lse_in, norm_row, mass, mass_in, mass_y, mass_in2, den,
    load_sem, emb_send, emb_recv, lse_send, lse_recv, a_send, a_recv, b_send, b_recv, c_send, c_recv,
    mass_send, mass_recv,
):
    dp = lax.axis_index("dp")
    x = lax.axis_index("cent")
    y, z, core = dp // 8, lax.rem(dp // 2, SIDE), lax.rem(dp, 2)

    def device(dx, dy, dz, dc):
        return {
            "dp": (lax.rem(y + dy, SIDE) * SIDE + lax.rem(z + dz, SIDE)) * 2 + lax.rem(core + dc, 2),
            "cent": lax.rem(x + dx, SIDE),
        }

    def along(axis, d, dc):
        return device(*[d if a == axis else 0 for a in range(3)], dc)

    def send(src, dst, send_sem, recv_sem, target):
        pltpu.make_async_remote_copy(
            src_ref=src, dst_ref=dst, send_sem=send_sem, recv_sem=recv_sem, device_id=target, device_id_type=MESH
        ).start()

    def wait(ref, sem):
        pltpu.make_async_copy(ref, ref, sem).wait()

    loads = [
        pltpu.make_async_copy(e_hbm, emb.at[pl.ds(0, ROWS)], load_sem.at[0]),
        pltpu.make_async_copy(c_hbm.at[pl.ds(core * HALF, HALF)], cent.at[0], load_sem.at[1]),
    ]
    for copy in loads:
        copy.start()
    c_other = pltpu.make_async_copy(c_hbm.at[pl.ds((1 - core) * HALF, HALF)], cent.at[1], load_sem.at[2])

    barrier = pltpu.get_barrier_semaphore()
    for d, dc in OTHERS:
        for axis in range(3):
            if d or axis == 0:
                pl.semaphore_signal(barrier, inc=1, device_id=along(axis, d, dc), device_id_type=MESH)

    def statistics(tile, top, total):
        for j in range(0, TILE, 64):
            part = tile[j : j + 64].reshape(8, 8, BLOCK)
            high = part.max(0)
            if top is None:
                total = jnp.exp(part - high[None]).sum(0)
            else:
                high = jnp.maximum(top, high)
                total = total * jnp.exp(top - high) + jnp.exp(part - high[None]).sum(0)
            top = high
        return top, total

    def row_lse(b, top, total):
        high = jnp.max(top, axis=0, keepdims=True)
        value = high + jnp.log(jnp.sum(total * jnp.exp(top - high), axis=0, keepdims=True))
        lse[b // 4, pl.ds(2 * lax.rem(b, 4), 1)] = value[:, 0:128]
        lse[b // 4, pl.ds(2 * lax.rem(b, 4) + 1, 1)] = value[:, 128:256]

    def send_lse(group):
        for j, (d, dc) in enumerate(OTHERS):
            send(lse.at[group], lse_in.at[group ^ dc, j], lse_send, lse_recv.at[group ^ dc], along(0, d, dc))

    def send_emb():
        for h in range(2):
            part = pl.ds(h * 512, 512)
            send(emb.at[part], emb.at[pl.ds(ROWS + h * 512, 512)], emb_send, emb_recv.at[h], device(0, 0, 0, 1))

    def norms(group):
        wait(lse_in.at[group], lse_recv.at[group])
        parts = [lse[group]] + [lse_in[group, j] for j in range(7)]
        top = parts[0]
        for part in parts[1:]:
            top = jnp.maximum(top, part)
        total = jnp.zeros_like(top)
        for part in parts:
            total = total + jnp.exp(part - top)
        norm = top + jnp.log(total)
        if group == 0:
            norm_ref[...] = norm
        for j in range(8):
            at = group * ROWS + j * 128
            norm_row[0:1, at : at + 128] = norm[j : j + 1]

    def take_previous(m, carry):
        at = pl.multiple_of((m % N_CHUNKS) * CHUNK, CHUNK)
        columns = pl.ds(pl.multiple_of(dp // 4 * 128, 128), 128)
        previous[m // N_CHUNKS, m % N_CHUNKS] = cent[m // N_CHUNKS, pl.ds(at, CHUNK), columns].T
        return carry

    def score_block(b):
        at = pl.multiple_of(b * BLOCK, BLOCK)
        rows = emb[pl.ds(at, BLOCK)]
        emb2[...] = rows * BF16(2)
        top = total = None
        for m in range(HALF // TILE):
            tile = lax.dot_general(
                cent[0, m * TILE : (m + 1) * TILE], emb2[...], (((1,), (1,)), ((), ())), preferred_element_type=F32
            )
            scores[b, m * TILE : (m + 1) * TILE] = tile
            top, total = statistics(tile, top, total)
        row_lse(b, top, total)
        emb_t[0:D, pl.ds(at, BLOCK)] = rows.T

    def score_step(q, carry):
        @pl.when(q == 1)
        def _():
            c_other.start()
            pl.semaphore_wait(barrier, 19)
            send_emb()

        for h in range(2):

            @pl.when(q == 2 + h)
            def _():
                wait(emb.at[pl.ds(ROWS + h * 512, 512)], emb_recv.at[h])

        for b in range(2):
            score_block(2 * q + b)

        @pl.when(q == 1)
        def _():
            send_lse(0)

        return carry

    emb_t[D : D + 16, :] = jnp.ones((16, 2 * ROWS), BF16)
    for copy in loads:
        copy.wait()
    lax.fori_loop(0, 4, score_step, 0)
    send_lse(1)
    c_other.wait()
    lax.fori_loop(0, 2 * N_CHUNKS, take_previous, 0)
    norms(0)
    norms(1)

    def exponentials(i, slot):
        for b in range(N_BLOCKS):
            norm = norm_row[0:1, b * BLOCK : (b + 1) * BLOCK]
            for j in range(0, CHUNK, 32):
                at = pl.multiple_of(i * CHUNK + j, 32)
                resp[slot, j : j + 32, b * BLOCK : (b + 1) * BLOCK] = jnp.exp(
                    scores[b, pl.ds(at, 32)] - norm
                ).astype(BF16)

    def product(i, slot):
        sums = lax.dot_general(
            emb_t[...], resp[slot], (((1,), (1,)), ((), ())), preferred_element_type=F32
        )
        for yy in range(SIDE):
            for zz in range(SIDE):
                at = (yy * SIDE + zz) * CHIP_COLS
                value = sums[at : at + CHIP_COLS].astype(BF16)
                if slot == 0:
                    weighted[i, yy, zz] = value
                else:
                    weighted[i, zz, yy] = value
        for k in range(2):
            mass[pl.ds(2 * i + k, 1)] = sums[D : D + 1, k * 128 : (k + 1) * 128]

    def places(slot):
        return (1, y, 2, z) if slot == 0 else (2, z, 1, y)

    def send_a(i, slot):
        axis, p, _, _ = places(slot)
        up, down, far = lax.rem(p + 1, SIDE), lax.rem(p + 3, SIDE), lax.rem(p + 2, SIDE)
        to_up, to_down = along(axis, 1, 0), along(axis, 3, 0)
        lo, hi = pl.ds(0, 2), pl.ds(2, 2)
        send(weighted.at[i, far, lo], gather_a.at[i, 0, 0], a_send, a_recv.at[i, 0], to_up)
        send(weighted.at[i, far, hi], gather_a.at[i, 0, 1], a_send, a_recv.at[i, 0], to_down)
        send(weighted.at[i, up, hi], gather_a.at[i, 1, 0], a_send, a_recv.at[i, 1], to_up)
        send(weighted.at[i, down, lo], gather_a.at[i, 1, 1], a_send, a_recv.at[i, 1], to_down)

    def relay_sums(i, slot):
        _, p, _, _ = places(slot)
        up, down = lax.rem(p + 1, SIDE), lax.rem(p + 3, SIDE)
        wait(gather_a.at[i, 0], a_recv.at[i, 0])
        relay[i, 0] = (weighted[i, up, 0:2].astype(F32) + gather_a[i, 0, 0].astype(F32)).astype(BF16)
        relay[i, 1] = (weighted[i, down, 2:4].astype(F32) + gather_a[i, 0, 1].astype(F32)).astype(BF16)

    def send_b(i, slot):
        axis, _, _, _ = places(slot)
        send(relay.at[i, 0], gather_b.at[i, 0], b_send, b_recv.at[i], along(axis, 1, 0))
        send(relay.at[i, 1], gather_b.at[i, 1], b_send, b_recv.at[i], along(axis, 3, 0))

    def second_sums(i, slot):
        _, p, _, _ = places(slot)
        wait(gather_a.at[i, 1], a_recv.at[i, 1])
        wait(gather_b.at[i], b_recv.at[i])
        low = weighted[i, p, 0:2].astype(F32) + gather_b[i, 0].astype(F32) + gather_a[i, 1, 1].astype(F32)
        high = weighted[i, p, 2:4].astype(F32) + gather_b[i, 1].astype(F32) + gather_a[i, 1, 0].astype(F32)
        second[i, 0:2] = low.astype(BF16).reshape(2, 2, DEV_COLS, CHUNK)
        second[i, 2:4] = high.astype(BF16).reshape(2, 2, DEV_COLS, CHUNK)

    def send_c(i, slot):
        _, _, axis, q = places(slot)
        for j, (d, dc) in enumerate(OTHERS):
            send(
                second.at[i, lax.rem(q + d, SIDE), lax.rem(core + dc, 2)], gather_c.at[i, j],
                c_send, c_recv.at[i], along(axis, d, dc),
            )

    def finish(i, slot):
        _, _, _, q = places(slot)
        wait(gather_c.at[i], c_recv.at[i])
        own = pl.ds(pl.multiple_of(lax.rem(dp, 4) * DEV_COLS, DEV_COLS), DEV_COLS)
        for h in range(2):
            if h == 0:
                total = second[i, q, core].astype(F32)
                for j in range(3):
                    total = total + gather_c[i, j].astype(F32)
            else:
                total = gather_c[i, 3].astype(F32)
                for j in range(4, 7):
                    total = total + gather_c[i, j].astype(F32)
            total = total + previous[h, i, own].astype(F32)
            for k in range(2):
                part = slice(k * 128, (k + 1) * 128)
                at = pl.multiple_of(lax.rem(core + h, 2) * HALF + i * CHUNK + k * 128, 128)
                out_ref[:, pl.ds(at, 128)] = (
                    total[:, part] / den[h, pl.ds(2 * i + k, 1)]
                ).astype(BF16)

    def send_mass(stage):
        if stage == 0:
            for d in range(1, SIDE):
                send(mass, mass_in.at[d - 1], mass_send, mass_recv.at[0], along(1, d, 0))
        elif stage == 1:
            wait(mass_in, mass_recv.at[0])
            mass_y[...] = mass[...] + mass_in[0] + mass_in[1] + mass_in[2]
            for j, (d, dc) in enumerate(OTHERS):
                send(mass_y, mass_in2.at[j], mass_send, mass_recv.at[1], along(2, d, dc))
        else:
            wait(mass_in2, mass_recv.at[1])
            den[0] = mass_y[...] + mass_in2[0] + mass_in2[1] + mass_in2[2] + 1.0
            den[1] = mass_in2[3] + mass_in2[4] + mass_in2[5] + mass_in2[6] + 1.0

    def sums_step(j, carry):
        product(2 * j, 0)
        exponentials(2 * j + 1, 1)
        product(2 * j + 1, 1)
        exponentials(jnp.minimum(2 * j + 2, N_CHUNKS - 1), 0)
        send_a(2 * j, 0)
        send_a(2 * j + 1, 1)
        return carry

    def pair(*steps):
        def both(j, carry):
            for step in steps:
                step(2 * j, 0)
                step(2 * j + 1, 1)
            return carry

        lax.fori_loop(0, N_CHUNKS // 2, both, 0)

    exponentials(0, 0)
    lax.fori_loop(0, N_CHUNKS // 2, sums_step, 0)
    send_mass(0)
    pair(relay_sums, send_b)
    send_mass(1)
    pair(second_sums, send_c)
    send_mass(2)
    pair(finish)
    wait(emb.at[pl.ds(ROWS, ROWS)], emb_send)
    wait(lse_in, lse_send)
    wait(gather_a, a_send)
    wait(gather_b, b_send)
    wait(mass_in, mass_send)
    wait(mass_in2, mass_send)
    wait(gather_c, c_send)


def per_device(embeddings, centroids):
    dma = pltpu.SemaphoreType.DMA
    norm, out = pl.pallas_call(
        kernel,
        out_shape=(
            jax.ShapeDtypeStruct((8, 128), F32),
            jax.ShapeDtypeStruct((DEV_COLS, CENT), BF16),
        ),
        in_specs=[pl.BlockSpec(memory_space=pl.ANY)] * 2,
        out_specs=(pl.BlockSpec(memory_space=pltpu.VMEM),) * 2,
        scratch_shapes=[
            pltpu.VMEM((2 * ROWS, D), BF16),
            pltpu.VMEM((BLOCK, D), BF16),
            pltpu.VMEM((D + 16, 2 * ROWS), BF16),
            pltpu.VMEM((2, HALF, D), BF16),
            pltpu.VMEM((N_BLOCKS, HALF, BLOCK), F32),
            pltpu.VMEM((2, CHUNK, 2 * ROWS), BF16),
            pltpu.VMEM((N_CHUNKS, SIDE, SIDE, CHIP_COLS, CHUNK), BF16),
            pltpu.VMEM((N_CHUNKS, 2, 2, CHIP_COLS, CHUNK), BF16),
            pltpu.VMEM((N_CHUNKS, 2, 2, 2, CHIP_COLS, CHUNK), BF16),
            pltpu.VMEM((N_CHUNKS, 2, 2, CHIP_COLS, CHUNK), BF16),
            pltpu.VMEM((N_CHUNKS, SIDE, 2, DEV_COLS, CHUNK), BF16),
            pltpu.VMEM((N_CHUNKS, 7, DEV_COLS, CHUNK), BF16),
            pltpu.VMEM((2, N_CHUNKS, 128, CHUNK), BF16),
            pltpu.VMEM((2, 8, 128), F32),
            pltpu.VMEM((2, 7, 8, 128), F32),
            pltpu.VMEM((1, 2 * ROWS), F32),
            pltpu.VMEM((16, 128), F32),
            pltpu.VMEM((3, 16, 128), F32),
            pltpu.VMEM((16, 128), F32),
            pltpu.VMEM((7, 16, 128), F32),
            pltpu.VMEM((2, 16, 128), F32),
            dma((3,)),
            dma, dma((2,)),
            dma, dma((2,)),
            dma, dma((N_CHUNKS, 2)),
            dma, dma((N_CHUNKS,)),
            dma, dma((N_CHUNKS,)),
            dma, dma((2,)),
        ],
        compiler_params=pltpu.CompilerParams(
            collective_id=0, has_side_effects=True, vmem_limit_bytes=60 * 2**20
        ),
    )(embeddings, centroids)
    return norm.reshape(ROWS), out.T


def solution(mesh):
    return jax.shard_map(
        per_device,
        mesh=mesh,
        in_specs=(P("dp", None), P("cent", None)),
        out_specs=(P("dp"), P("cent", "dp")),
        check_vma=False,
    )
```

```python
import jax
import jax.numpy as jnp
from jax import lax
from jax.experimental import pallas as pl
from jax.experimental.pallas import tpu as pltpu
from jax.sharding import PartitionSpec as P

MESH = pl.DeviceIdType.MESH
F32, BF16 = jnp.float32, jnp.bfloat16

SIDE = 4
D = 1024
ROWS = 1024
CENT = 4096
HALF = CENT // 2
BLOCK = 256
TILE = 256
CHUNK = 256
N_BLOCKS = 2 * ROWS // BLOCK
N_CHUNKS = HALF // CHUNK
CHIP_COLS = D // (SIDE * SIDE)
DEV_COLS = CHIP_COLS // 2

OTHERS = [(d, c) for c in range(2) for d in range(SIDE) if (d, c) != (0, 0)]
FAR_FIRST = (1, 5, 0, 2, 4, 6, 3)


def kernel(
    e_hbm, c_hbm, norm_ref, out_ref,
    emb, emb2, emb_t, cent, scores, resp, weighted, relay, gather_a, gather_b, second, gather_c, previous,
    lse, lse_in, norm_row, mass, mass_in, mass_y, mass_in2, den,
    load_sem, emb_send, emb_recv, lse_send, lse_recv, a_send, a_recv, b_send, b_recv, c_send, c_recv,
    mass_send, mass_recv,
):
    dp = lax.axis_index("dp")
    x = lax.axis_index("cent")
    y, z, core = dp // 8, lax.rem(dp // 2, SIDE), lax.rem(dp, 2)

    def device(dx, dy, dz, dc):
        return {
            "dp": (lax.rem(y + dy, SIDE) * SIDE + lax.rem(z + dz, SIDE)) * 2 + lax.rem(core + dc, 2),
            "cent": lax.rem(x + dx, SIDE),
        }

    def along(axis, d, dc):
        return device(*[d if a == axis else 0 for a in range(3)], dc)

    def send(src, dst, send_sem, recv_sem, target):
        pltpu.make_async_remote_copy(
            src_ref=src, dst_ref=dst, send_sem=send_sem, recv_sem=recv_sem, device_id=target, device_id_type=MESH
        ).start()

    def wait(ref, sem):
        pltpu.make_async_copy(ref, ref, sem).wait()

    loads = [
        pltpu.make_async_copy(e_hbm.at[pl.ds(0, 512)], emb.at[pl.ds(0, 512)], load_sem.at[0]),
        pltpu.make_async_copy(c_hbm.at[pl.ds(core * HALF, HALF)], cent.at[0], load_sem.at[1]),
        pltpu.make_async_copy(e_hbm.at[pl.ds(512, 512)], emb.at[pl.ds(512, 512)], load_sem.at[3]),
    ]
    for copy in loads:
        copy.start()
    c_other = pltpu.make_async_copy(c_hbm.at[pl.ds((1 - core) * HALF, HALF)], cent.at[1], load_sem.at[2])

    barrier = pltpu.get_barrier_semaphore()
    for d, dc in OTHERS:
        for axis in range(3):
            if d or axis == 0:
                pl.semaphore_signal(barrier, inc=1, device_id=along(axis, d, dc), device_id_type=MESH)

    def statistics(tile, top, total):
        for j in range(0, TILE, 64):
            part = tile[j : j + 64].reshape(8, 8, BLOCK)
            high = part.max(0)
            if top is None:
                total = jnp.exp(part - high[None]).sum(0)
            else:
                high = jnp.maximum(top, high)
                total = total * jnp.exp(top - high) + jnp.exp(part - high[None]).sum(0)
            top = high
        return top, total

    def row_lse(b, top, total):
        high = jnp.max(top, axis=0, keepdims=True)
        value = high + jnp.log(jnp.sum(total * jnp.exp(top - high), axis=0, keepdims=True))
        lse[b // 4, pl.ds(2 * lax.rem(b, 4), 1)] = value[:, 0:128]
        lse[b // 4, pl.ds(2 * lax.rem(b, 4) + 1, 1)] = value[:, 128:256]

    def send_lse(group):
        for j in FAR_FIRST:
            d, dc = OTHERS[j]
            send(lse.at[group], lse_in.at[group ^ dc, j], lse_send, lse_recv.at[group ^ dc], along(0, d, dc))

    def send_emb():
        for h in range(2):
            part = pl.ds(h * 512, 512)
            send(emb.at[part], emb.at[pl.ds(ROWS + h * 512, 512)], emb_send, emb_recv.at[h], device(0, 0, 0, 1))

    def norms(group):
        wait(lse_in.at[group], lse_recv.at[group])
        parts = [lse[group]] + [lse_in[group, j] for j in range(7)]
        top = parts[0]
        for part in parts[1:]:
            top = jnp.maximum(top, part)
        total = jnp.zeros_like(top)
        for part in parts:
            total = total + jnp.exp(part - top)
        norm = top + jnp.log(total)
        if group == 0:
            norm_ref[...] = norm
        for j in range(8):
            at = group * ROWS + j * 128
            norm_row[0:1, at : at + 128] = norm[j : j + 1]

    def take_previous(m, carry):
        at = pl.multiple_of((m % N_CHUNKS) * CHUNK, CHUNK)
        columns = pl.ds(pl.multiple_of(dp // 4 * 128, 128), 128)
        previous[m // N_CHUNKS, m % N_CHUNKS] = cent[m // N_CHUNKS, pl.ds(at, CHUNK), columns].T
        return carry

    def score_block(b):
        at = pl.multiple_of(b * BLOCK, BLOCK)
        rows = emb[pl.ds(at, BLOCK)]
        emb2[...] = rows * BF16(2)
        top = total = None
        for m in range(HALF // TILE):
            tile = lax.dot_general(
                cent[0, m * TILE : (m + 1) * TILE], emb2[...], (((1,), (1,)), ((), ())), preferred_element_type=F32
            )
            scores[b, m * TILE : (m + 1) * TILE] = tile
            top, total = statistics(tile, top, total)
        row_lse(b, top, total)
        emb_t[0:D, pl.ds(at, BLOCK)] = rows.T

    def score_step(q, carry):
        @pl.when(q == 1)
        def _():
            loads[2].wait()
            c_other.start()
            pl.semaphore_wait(barrier, 19)
            send_emb()

        for h in range(2):

            @pl.when(q == 2 + h)
            def _():
                wait(emb.at[pl.ds(ROWS + h * 512, 512)], emb_recv.at[h])

        for b in range(2):
            score_block(2 * q + b)

        @pl.when(q == 1)
        def _():
            send_lse(0)

        return carry

    emb_t[D : D + 16, :] = jnp.ones((16, 2 * ROWS), BF16)
    for copy in loads[:2]:
        copy.wait()
    lax.fori_loop(0, 4, score_step, 0)
    send_lse(1)
    c_other.wait()
    lax.fori_loop(0, 2 * N_CHUNKS, take_previous, 0)
    norms(0)
    norms(1)

    def exponentials(i, slot):
        for b in range(N_BLOCKS):
            norm = norm_row[0:1, b * BLOCK : (b + 1) * BLOCK]
            for j in range(0, CHUNK, 32):
                at = pl.multiple_of(i * CHUNK + j, 32)
                resp[slot, j : j + 32, b * BLOCK : (b + 1) * BLOCK] = jnp.exp(
                    scores[b, pl.ds(at, 32)] - norm
                ).astype(BF16)

    def product(i, slot):
        sums = lax.dot_general(
            emb_t[...], resp[slot], (((1,), (1,)), ((), ())), preferred_element_type=F32
        )
        for yy in range(SIDE):
            for zz in range(SIDE):
                at = (yy * SIDE + zz) * CHIP_COLS
                value = sums[at : at + CHIP_COLS].astype(BF16)
                if slot == 0:
                    weighted[i, yy, zz] = value
                else:
                    weighted[i, zz, yy] = value
        for k in range(2):
            mass[pl.ds(2 * i + k, 1)] = sums[D : D + 1, k * 128 : (k + 1) * 128]

    def places(slot):
        return (1, y, 2, z) if slot == 0 else (2, z, 1, y)

    def copies_a(i, slot):
        axis, p, _, _ = places(slot)
        up, down, far = lax.rem(p + 1, SIDE), lax.rem(p + 3, SIDE), lax.rem(p + 2, SIDE)
        to_up, to_down = along(axis, 1, 0), along(axis, 3, 0)
        lo, hi = pl.ds(0, 2), pl.ds(2, 2)
        return [
            (weighted.at[i, far, lo], gather_a.at[i, 0, 0], a_send, a_recv.at[i, 0], to_up),
            (weighted.at[i, far, hi], gather_a.at[i, 0, 1], a_send, a_recv.at[i, 0], to_down),
            (weighted.at[i, up, hi], gather_a.at[i, 1, 0], a_send, a_recv.at[i, 1], to_up),
            (weighted.at[i, down, lo], gather_a.at[i, 1, 1], a_send, a_recv.at[i, 1], to_down),
        ]

    def relay_sums(i, slot):
        _, p, _, _ = places(slot)
        up, down = lax.rem(p + 1, SIDE), lax.rem(p + 3, SIDE)
        wait(gather_a.at[i, 0], a_recv.at[i, 0])
        relay[i, 0] = (weighted[i, up, 0:2].astype(F32) + gather_a[i, 0, 0].astype(F32)).astype(BF16)
        relay[i, 1] = (weighted[i, down, 2:4].astype(F32) + gather_a[i, 0, 1].astype(F32)).astype(BF16)

    def copies_b(i, slot):
        axis, _, _, _ = places(slot)
        return [
            (relay.at[i, 0], gather_b.at[i, 0], b_send, b_recv.at[i], along(axis, 1, 0)),
            (relay.at[i, 1], gather_b.at[i, 1], b_send, b_recv.at[i], along(axis, 3, 0)),
        ]

    def second_sums(i, slot):
        _, p, _, _ = places(slot)
        wait(gather_a.at[i, 1], a_recv.at[i, 1])
        wait(gather_b.at[i], b_recv.at[i])
        low = weighted[i, p, 0:2].astype(F32) + gather_b[i, 0].astype(F32) + gather_a[i, 1, 1].astype(F32)
        high = weighted[i, p, 2:4].astype(F32) + gather_b[i, 1].astype(F32) + gather_a[i, 1, 0].astype(F32)
        second[i, 0:2] = low.astype(BF16).reshape(2, 2, DEV_COLS, CHUNK)
        second[i, 2:4] = high.astype(BF16).reshape(2, 2, DEV_COLS, CHUNK)

    def copies_c(i, slot):
        _, _, axis, q = places(slot)
        copies = []
        for j in FAR_FIRST:
            d, dc = OTHERS[j]
            part = second.at[i, lax.rem(q + d, SIDE), lax.rem(core + dc, 2)]
            copies.append((part, gather_c.at[i, j], c_send, c_recv.at[i], along(axis, d, dc)))
        return copies

    def send_pair(copies, j):
        for both in zip(copies(2 * j, 0), copies(2 * j + 1, 1)):
            for copy in both:
                send(*copy)

    def finish(i, slot):
        _, _, _, q = places(slot)
        wait(gather_c.at[i], c_recv.at[i])
        own = pl.ds(pl.multiple_of(lax.rem(dp, 4) * DEV_COLS, DEV_COLS), DEV_COLS)
        for h in range(2):
            if h == 0:
                total = second[i, q, core].astype(F32)
                for j in range(3):
                    total = total + gather_c[i, j].astype(F32)
            else:
                total = gather_c[i, 3].astype(F32)
                for j in range(4, 7):
                    total = total + gather_c[i, j].astype(F32)
            total = total + previous[h, i, own].astype(F32)
            for k in range(2):
                part = slice(k * 128, (k + 1) * 128)
                at = pl.multiple_of(lax.rem(core + h, 2) * HALF + i * CHUNK + k * 128, 128)
                out_ref[:, pl.ds(at, 128)] = (
                    total[:, part] / den[h, pl.ds(2 * i + k, 1)]
                ).astype(BF16)

    def send_mass(stage):
        if stage == 0:
            for d in range(1, SIDE):
                send(mass, mass_in.at[d - 1], mass_send, mass_recv.at[0], along(1, d, 0))
        elif stage == 1:
            wait(mass_in, mass_recv.at[0])
            mass_y[...] = mass[...] + mass_in[0] + mass_in[1] + mass_in[2]
            for j, (d, dc) in enumerate(OTHERS):
                send(mass_y, mass_in2.at[j], mass_send, mass_recv.at[1], along(2, d, dc))
        else:
            wait(mass_in2, mass_recv.at[1])
            den[0] = mass_y[...] + mass_in2[0] + mass_in2[1] + mass_in2[2] + 1.0
            den[1] = mass_in2[3] + mass_in2[4] + mass_in2[5] + mass_in2[6] + 1.0

    def sums_step(j, carry):
        product(2 * j, 0)
        exponentials(2 * j + 1, 1)
        product(2 * j + 1, 1)
        exponentials(jnp.minimum(2 * j + 2, N_CHUNKS - 1), 0)
        send_pair(copies_a, j)
        return carry

    def pair(step, copies=None):
        def both(j, carry):
            step(2 * j, 0)
            step(2 * j + 1, 1)
            if copies is not None:
                send_pair(copies, j)
            return carry

        lax.fori_loop(0, N_CHUNKS // 2, both, 0)

    exponentials(0, 0)
    lax.fori_loop(0, N_CHUNKS // 2, sums_step, 0)
    send_mass(0)
    pair(relay_sums, copies_b)
    send_mass(1)
    pair(second_sums, copies_c)
    send_mass(2)
    pair(finish)
    wait(emb.at[pl.ds(ROWS, ROWS)], emb_send)
    wait(lse_in, lse_send)
    wait(gather_a, a_send)
    wait(gather_b, b_send)
    wait(mass_in, mass_send)
    wait(mass_in2, mass_send)
    wait(gather_c, c_send)


def per_device(embeddings, centroids):
    dma = pltpu.SemaphoreType.DMA
    norm, out = pl.pallas_call(
        kernel,
        out_shape=(
            jax.ShapeDtypeStruct((8, 128), F32),
            jax.ShapeDtypeStruct((DEV_COLS, CENT), BF16),
        ),
        in_specs=[pl.BlockSpec(memory_space=pl.ANY)] * 2,
        out_specs=(pl.BlockSpec(memory_space=pltpu.VMEM),) * 2,
        scratch_shapes=[
            pltpu.VMEM((2 * ROWS, D), BF16),
            pltpu.VMEM((BLOCK, D), BF16),
            pltpu.VMEM((D + 16, 2 * ROWS), BF16),
            pltpu.VMEM((2, HALF, D), BF16),
            pltpu.VMEM((N_BLOCKS, HALF, BLOCK), F32),
            pltpu.VMEM((2, CHUNK, 2 * ROWS), BF16),
            pltpu.VMEM((N_CHUNKS, SIDE, SIDE, CHIP_COLS, CHUNK), BF16),
            pltpu.VMEM((N_CHUNKS, 2, 2, CHIP_COLS, CHUNK), BF16),
            pltpu.VMEM((N_CHUNKS, 2, 2, 2, CHIP_COLS, CHUNK), BF16),
            pltpu.VMEM((N_CHUNKS, 2, 2, CHIP_COLS, CHUNK), BF16),
            pltpu.VMEM((N_CHUNKS, SIDE, 2, DEV_COLS, CHUNK), BF16),
            pltpu.VMEM((N_CHUNKS, 7, DEV_COLS, CHUNK), BF16),
            pltpu.VMEM((2, N_CHUNKS, 128, CHUNK), BF16),
            pltpu.VMEM((2, 8, 128), F32),
            pltpu.VMEM((2, 7, 8, 128), F32),
            pltpu.VMEM((1, 2 * ROWS), F32),
            pltpu.VMEM((16, 128), F32),
            pltpu.VMEM((3, 16, 128), F32),
            pltpu.VMEM((16, 128), F32),
            pltpu.VMEM((7, 16, 128), F32),
            pltpu.VMEM((2, 16, 128), F32),
            dma((4,)),
            dma, dma((2,)),
            dma, dma((2,)),
            dma, dma((N_CHUNKS, 2)),
            dma, dma((N_CHUNKS,)),
            dma, dma((N_CHUNKS,)),
            dma, dma((2,)),
        ],
        compiler_params=pltpu.CompilerParams(
            collective_id=0, has_side_effects=True, vmem_limit_bytes=60 * 2**20
        ),
    )(embeddings, centroids)
    return norm.reshape(ROWS), out.T


def solution(mesh):
    return jax.shard_map(
        per_device,
        mesh=mesh,
        in_specs=(P("dp", None), P("cent", None)),
        out_specs=(P("dp"), P("cent", "dp")),
        check_vma=False,
    )
```

```python
import jax
import jax.numpy as jnp
from jax import lax
from jax.experimental import pallas as pl
from jax.experimental.pallas import tpu as pltpu
from jax.sharding import PartitionSpec as P

MESH = pl.DeviceIdType.MESH
F32, BF16 = jnp.float32, jnp.bfloat16

SIDE = 4
D = 1024
ROWS = 1024
CENT = 4096
HALF = CENT // 2
BLOCK = 256
TILE = 256
CHUNK = 256
N_BLOCKS = 2 * ROWS // BLOCK
N_CHUNKS = HALF // CHUNK
CHIP_COLS = D // (SIDE * SIDE)
DEV_COLS = CHIP_COLS // 2

OTHERS = [(d, c) for c in range(2) for d in range(SIDE) if (d, c) != (0, 0)]
FAR_FIRST = (1, 5, 0, 2, 4, 6, 3)


def kernel(
    e_hbm, c_hbm, norm_ref, out_ref,
    emb, emb2, emb_t, cent, scores, resp, weighted, relay, gather_a, gather_b, second, gather_c, previous,
    lse, lse_in, norm_row, mass, mass_in, mass_y, mass_in2, den,
    load_sem, emb_send, emb_recv, lse_send, lse_recv, a_send, a_recv, b_send, b_recv, c_send, c_recv,
    mass_send, mass_recv,
):
    dp = lax.axis_index("dp")
    x = lax.axis_index("cent")
    y, z, core = dp // 8, lax.rem(dp // 2, SIDE), lax.rem(dp, 2)

    def device(dx, dy, dz, dc):
        return {
            "dp": (lax.rem(y + dy, SIDE) * SIDE + lax.rem(z + dz, SIDE)) * 2 + lax.rem(core + dc, 2),
            "cent": lax.rem(x + dx, SIDE),
        }

    def along(axis, d, dc):
        return device(*[d if a == axis else 0 for a in range(3)], dc)

    def send(src, dst, send_sem, recv_sem, target):
        pltpu.make_async_remote_copy(
            src_ref=src, dst_ref=dst, send_sem=send_sem, recv_sem=recv_sem, device_id=target, device_id_type=MESH
        ).start()

    def wait(ref, sem):
        pltpu.make_async_copy(ref, ref, sem).wait()

    loads = [
        pltpu.make_async_copy(e_hbm.at[pl.ds(0, 512)], emb.at[pl.ds(0, 512)], load_sem.at[0]),
        pltpu.make_async_copy(c_hbm.at[pl.ds(core * HALF, HALF)], cent.at[0], load_sem.at[1]),
        pltpu.make_async_copy(e_hbm.at[pl.ds(512, 512)], emb.at[pl.ds(512, 512)], load_sem.at[3]),
    ]
    for copy in loads:
        copy.start()
    c_other = pltpu.make_async_copy(c_hbm.at[pl.ds((1 - core) * HALF, HALF)], cent.at[1], load_sem.at[2])

    barrier = pltpu.get_barrier_semaphore()
    for d, dc in OTHERS:
        for axis in range(3):
            if d or axis == 0:
                pl.semaphore_signal(barrier, inc=1, device_id=along(axis, d, dc), device_id_type=MESH)

    def statistics(tile, top, total):
        for j in range(0, TILE, 64):
            part = tile[j : j + 64].reshape(8, 8, BLOCK)
            high = part.max(0)
            if top is None:
                total = jnp.exp(part - high[None]).sum(0)
            else:
                high = jnp.maximum(top, high)
                total = total * jnp.exp(top - high) + jnp.exp(part - high[None]).sum(0)
            top = high
        return top, total

    def row_lse(b, top, total):
        high = jnp.max(top, axis=0, keepdims=True)
        value = high + jnp.log(jnp.sum(total * jnp.exp(top - high), axis=0, keepdims=True))
        lse[b // 4, pl.ds(2 * lax.rem(b, 4), 1)] = value[:, 0:128]
        lse[b // 4, pl.ds(2 * lax.rem(b, 4) + 1, 1)] = value[:, 128:256]

    def send_lse(group):
        for j in FAR_FIRST:
            d, dc = OTHERS[j]
            send(lse.at[group], lse_in.at[group ^ dc, j], lse_send, lse_recv.at[group ^ dc], along(0, d, dc))

    def send_emb():
        for h in range(2):
            part = pl.ds(h * 512, 512)
            send(emb.at[part], emb.at[pl.ds(ROWS + h * 512, 512)], emb_send, emb_recv.at[h], device(0, 0, 0, 1))

    def norms(group):
        wait(lse_in.at[group], lse_recv.at[group])
        parts = [lse[group]] + [lse_in[group, j] for j in range(7)]
        top = parts[0]
        for part in parts[1:]:
            top = jnp.maximum(top, part)
        total = jnp.zeros_like(top)
        for part in parts:
            total = total + jnp.exp(part - top)
        norm = top + jnp.log(total)
        if group == 0:
            norm_ref[...] = norm
        for j in range(8):
            at = group * ROWS + j * 128
            norm_row[0:1, at : at + 128] = norm[j : j + 1]

    def take_previous(m, carry):
        at = pl.multiple_of((m % N_CHUNKS) * CHUNK, CHUNK)
        columns = pl.ds(pl.multiple_of(dp // 4 * 128, 128), 128)
        previous[m // N_CHUNKS, m % N_CHUNKS] = cent[m // N_CHUNKS, pl.ds(at, CHUNK), columns].T
        return carry

    def score_block(b):
        at = pl.multiple_of(b * BLOCK, BLOCK)
        rows = emb[pl.ds(at, BLOCK)]
        emb2[...] = rows * BF16(2)
        top = total = None
        for m in range(HALF // TILE):
            tile = lax.dot_general(
                cent[0, m * TILE : (m + 1) * TILE], emb2[...], (((1,), (1,)), ((), ())), preferred_element_type=F32
            )
            scores[b, m * TILE : (m + 1) * TILE] = tile
            top, total = statistics(tile, top, total)
        row_lse(b, top, total)
        emb_t[0:D, pl.ds(at, BLOCK)] = rows.T

    def score_step(q, carry):
        @pl.when(q == 1)
        def _():
            loads[2].wait()
            c_other.start()
            pl.semaphore_wait(barrier, 19)
            send_emb()

        for h in range(2):

            @pl.when(q == 2 + h)
            def _():
                wait(emb.at[pl.ds(ROWS + h * 512, 512)], emb_recv.at[h])

        for b in range(2):
            score_block(2 * q + b)

        @pl.when(q == 1)
        def _():
            send_lse(0)

        return carry

    emb_t[D : D + 16, :] = jnp.ones((16, 2 * ROWS), BF16)
    for copy in loads[:2]:
        copy.wait()
    lax.fori_loop(0, 4, score_step, 0)
    send_lse(1)
    c_other.wait()
    lax.fori_loop(0, 2 * N_CHUNKS, take_previous, 0)
    norms(0)
    norms(1)

    def exponentials(i, slot):
        for b in range(N_BLOCKS):
            norm = norm_row[0:1, b * BLOCK : (b + 1) * BLOCK]
            for j in range(0, CHUNK, 32):
                at = pl.multiple_of(i * CHUNK + j, 32)
                resp[slot, j : j + 32, b * BLOCK : (b + 1) * BLOCK] = jnp.exp(
                    scores[b, pl.ds(at, 32)] - norm
                ).astype(BF16)

    def product(i, slot):
        sums = lax.dot_general(
            emb_t[...], resp[slot], (((1,), (1,)), ((), ())), preferred_element_type=F32
        )
        for yy in range(SIDE):
            for zz in range(SIDE):
                at = (yy * SIDE + zz) * CHIP_COLS
                value = sums[at : at + CHIP_COLS].astype(BF16)
                if slot == 0:
                    weighted[i, yy, zz] = value
                else:
                    weighted[i, zz, yy] = value
        for k in range(2):
            mass[pl.ds(2 * i + k, 1)] = sums[D : D + 1, k * 128 : (k + 1) * 128]

    def places(slot):
        return (1, y, 2, z) if slot == 0 else (2, z, 1, y)

    def copies_a(i, slot):
        axis, p, _, _ = places(slot)
        up, down, far = lax.rem(p + 1, SIDE), lax.rem(p + 3, SIDE), lax.rem(p + 2, SIDE)
        to_up, to_down = along(axis, 1, 0), along(axis, 3, 0)
        lo, hi = pl.ds(0, 2), pl.ds(2, 2)
        return [
            (weighted.at[i, far, lo], gather_a.at[i, 0, 0], a_send, a_recv.at[i, 0], to_up),
            (weighted.at[i, far, hi], gather_a.at[i, 0, 1], a_send, a_recv.at[i, 0], to_down),
            (weighted.at[i, up, hi], gather_a.at[i, 1, 0], a_send, a_recv.at[i, 1], to_up),
            (weighted.at[i, down, lo], gather_a.at[i, 1, 1], a_send, a_recv.at[i, 1], to_down),
        ]

    def relay_sums(i, slot):
        _, p, _, _ = places(slot)
        up, down = lax.rem(p + 1, SIDE), lax.rem(p + 3, SIDE)
        wait(gather_a.at[i, 0], a_recv.at[i, 0])
        relay[i, 0] = (weighted[i, up, 0:2].astype(F32) + gather_a[i, 0, 0].astype(F32)).astype(BF16)
        relay[i, 1] = (weighted[i, down, 2:4].astype(F32) + gather_a[i, 0, 1].astype(F32)).astype(BF16)

    def copies_b(i, slot):
        axis, _, _, _ = places(slot)
        return [
            (relay.at[i, 0], gather_b.at[i, 0], b_send, b_recv.at[i], along(axis, 1, 0)),
            (relay.at[i, 1], gather_b.at[i, 1], b_send, b_recv.at[i], along(axis, 3, 0)),
        ]

    def second_sums(i, slot):
        _, p, _, _ = places(slot)
        wait(gather_a.at[i, 1], a_recv.at[i, 1])
        wait(gather_b.at[i], b_recv.at[i])
        low = weighted[i, p, 0:2].astype(F32) + gather_b[i, 0].astype(F32) + gather_a[i, 1, 1].astype(F32)
        high = weighted[i, p, 2:4].astype(F32) + gather_b[i, 1].astype(F32) + gather_a[i, 1, 0].astype(F32)
        second[i, 0:2] = low.astype(BF16).reshape(2, 2, DEV_COLS, CHUNK)
        second[i, 2:4] = high.astype(BF16).reshape(2, 2, DEV_COLS, CHUNK)

    def copies_c(i, slot):
        _, _, axis, q = places(slot)
        copies = []
        for j in FAR_FIRST:
            d, dc = OTHERS[j]
            part = second.at[i, lax.rem(q + d, SIDE), lax.rem(core + dc, 2)]
            copies.append((part, gather_c.at[i, j], c_send, c_recv.at[i], along(axis, d, dc)))
        return copies

    def send_pair(copies, j):
        for both in zip(copies(2 * j, 0), copies(2 * j + 1, 1)):
            for copy in both:
                send(*copy)

    def finish(i, slot):
        _, _, _, q = places(slot)
        wait(gather_c.at[i], c_recv.at[i])
        own = pl.ds(pl.multiple_of(lax.rem(dp, 4) * DEV_COLS, DEV_COLS), DEV_COLS)
        for h in range(2):
            if h == 0:
                total = second[i, q, core].astype(F32)
                for j in range(3):
                    total = total + gather_c[i, j].astype(F32)
            else:
                total = gather_c[i, 3].astype(F32)
                for j in range(4, 7):
                    total = total + gather_c[i, j].astype(F32)
            total = total + previous[h, i, own].astype(F32)
            for k in range(2):
                part = slice(k * 128, (k + 1) * 128)
                at = pl.multiple_of(lax.rem(core + h, 2) * HALF + i * CHUNK + k * 128, 128)
                out_ref[:, pl.ds(at, 128)] = (
                    total[:, part] / den[h, pl.ds(2 * i + k, 1)]
                ).astype(BF16)

    def send_mass(stage):
        if stage == 0:
            for d in range(1, SIDE):
                send(mass, mass_in.at[d - 1], mass_send, mass_recv.at[0], along(1, d, 0))
        elif stage == 1:
            wait(mass_in, mass_recv.at[0])
            mass_y[...] = mass[...] + mass_in[0] + mass_in[1] + mass_in[2]
            for j, (d, dc) in enumerate(OTHERS):
                send(mass_y, mass_in2.at[j], mass_send, mass_recv.at[1], along(2, d, dc))
        else:
            wait(mass_in2, mass_recv.at[1])
            den[0] = mass_y[...] + mass_in2[0] + mass_in2[1] + mass_in2[2] + 1.0
            den[1] = mass_in2[3] + mass_in2[4] + mass_in2[5] + mass_in2[6] + 1.0

    def sums_step(j, carry):
        @pl.when(j == N_CHUNKS // 2 - 1)
        def _():
            relay_sums(0, 0)
            relay_sums(1, 1)
            send_pair(copies_b, 0)

        product(2 * j, 0)
        exponentials(2 * j + 1, 1)
        product(2 * j + 1, 1)
        exponentials(jnp.minimum(2 * j + 2, N_CHUNKS - 1), 0)
        send_pair(copies_a, j)
        return carry

    def pair(step, copies=None, first=0):
        def both(j, carry):
            step(2 * j, 0)
            step(2 * j + 1, 1)
            if copies is not None:
                send_pair(copies, j)
            return carry

        lax.fori_loop(first, N_CHUNKS // 2, both, 0)

    exponentials(0, 0)
    lax.fori_loop(0, N_CHUNKS // 2, sums_step, 0)
    send_mass(0)
    pair(relay_sums, copies_b, 1)
    send_mass(1)
    pair(second_sums, copies_c)
    send_mass(2)
    pair(finish)
    wait(emb.at[pl.ds(ROWS, ROWS)], emb_send)
    wait(lse_in, lse_send)
    wait(gather_a, a_send)
    wait(gather_b, b_send)
    wait(mass_in, mass_send)
    wait(mass_in2, mass_send)
    wait(gather_c, c_send)


def per_device(embeddings, centroids):
    dma = pltpu.SemaphoreType.DMA
    norm, out = pl.pallas_call(
        kernel,
        out_shape=(
            jax.ShapeDtypeStruct((8, 128), F32),
            jax.ShapeDtypeStruct((DEV_COLS, CENT), BF16),
        ),
        in_specs=[pl.BlockSpec(memory_space=pl.ANY)] * 2,
        out_specs=(pl.BlockSpec(memory_space=pltpu.VMEM),) * 2,
        scratch_shapes=[
            pltpu.VMEM((2 * ROWS, D), BF16),
            pltpu.VMEM((BLOCK, D), BF16),
            pltpu.VMEM((D + 16, 2 * ROWS), BF16),
            pltpu.VMEM((2, HALF, D), BF16),
            pltpu.VMEM((N_BLOCKS, HALF, BLOCK), F32),
            pltpu.VMEM((2, CHUNK, 2 * ROWS), BF16),
            pltpu.VMEM((N_CHUNKS, SIDE, SIDE, CHIP_COLS, CHUNK), BF16),
            pltpu.VMEM((N_CHUNKS, 2, 2, CHIP_COLS, CHUNK), BF16),
            pltpu.VMEM((N_CHUNKS, 2, 2, 2, CHIP_COLS, CHUNK), BF16),
            pltpu.VMEM((N_CHUNKS, 2, 2, CHIP_COLS, CHUNK), BF16),
            pltpu.VMEM((N_CHUNKS, SIDE, 2, DEV_COLS, CHUNK), BF16),
            pltpu.VMEM((N_CHUNKS, 7, DEV_COLS, CHUNK), BF16),
            pltpu.VMEM((2, N_CHUNKS, 128, CHUNK), BF16),
            pltpu.VMEM((2, 8, 128), F32),
            pltpu.VMEM((2, 7, 8, 128), F32),
            pltpu.VMEM((1, 2 * ROWS), F32),
            pltpu.VMEM((16, 128), F32),
            pltpu.VMEM((3, 16, 128), F32),
            pltpu.VMEM((16, 128), F32),
            pltpu.VMEM((7, 16, 128), F32),
            pltpu.VMEM((2, 16, 128), F32),
            dma((4,)),
            dma, dma((2,)),
            dma, dma((2,)),
            dma, dma((N_CHUNKS, 2)),
            dma, dma((N_CHUNKS,)),
            dma, dma((N_CHUNKS,)),
            dma, dma((2,)),
        ],
        compiler_params=pltpu.CompilerParams(
            collective_id=0, has_side_effects=True, vmem_limit_bytes=60 * 2**20
        ),
    )(embeddings, centroids)
    return norm.reshape(ROWS), out.T


def solution(mesh):
    return jax.shard_map(
        per_device,
        mesh=mesh,
        in_specs=(P("dp", None), P("cent", None)),
        out_specs=(P("dp"), P("cent", "dp")),
        check_vma=False,
    )
```
